32 devices in a mesh: grp: 2 (over x), row: 16 (over z, y, core).
Axes of the slice: x: 2, y: 2, z: 4, core: 2. Of those that a mesh axis runs over, the one named last changes fastest.
Arguments:
- pair_rep: bfloat16 [64, 32, 128], P(('grp', 'row')), parts along dimension 0, may hold values from -6 to 6
- residue_mask: int32 [64], P('grp'), parts along dimension 0, may hold values 0 or 1
- side_weights: bfloat16 [2, 5, 128, 128], replicated, may hold values from -0.5 to 0.5
- out_weights: bfloat16 [2, 128, 128], replicated, may hold values from -0.5 to 0.5
- norm_gains: float32 [2, 2, 128], replicated, may hold values from 0.1 to 1.9
Outputs:
- updated: bfloat16 [64, 32, 128], P(('grp', 'row')), parts along dimension 0
The draws below stay inside these ranges and needn't reach their ends.
There are 2 independent parts, one for each index of `grp`. The reference program is written for one: setup_inputs(seed, part) draws one part's arguments, and reference() takes and returns one part's arrays. A program takes and returns all parts, laid end to end along the dimension named above; an argument that names none is the same for every part. Nothing has to cross between parts.
All inputs are finite; a program needn't handle non-finite values.
Results may differ from the reference program's by a relative error of at most 0.013.
Values may be sent and summed in bfloat16 or wider, within the bound.
A program may use at most 64 MiB of HBM per device.

```python
import jax
import jax.numpy as jnp
from jax import lax

C = 128
N = 32


def plant(result, stream_key, low, high):
    index_at = [jax.random.randint(jax.random.fold_in(stream_key, axis), (), 0, length) for axis, length in enumerate(result.shape)]
    widest = result.shape.index(max(result.shape))
    beside = index_at[:widest] + [(index_at[widest] + 1) % result.shape[widest]] + index_at[widest + 1:]
    return result.at[tuple(index_at)].set(low).at[tuple(beside)].set(high)


def steps_of(stream_key, shape, cuts, low, high):
    def one(position, parts):
        draws = jax.random.uniform(jax.random.fold_in(jax.random.fold_in(stream_key, 6), position), (parts,), jnp.float32, low / len(cuts), high / len(cuts))
        return jnp.repeat(jnp.exp(draws), shape[position] // parts).reshape((-1,) + (1,) * (len(shape) - position - 1))

    level = one(*cuts[0])
    for cut in cuts[1:]:
        level = level * one(*cut)
    return level


def centred(rng, shape, scale, limit, cuts=(), dtype=jnp.bfloat16):
    array = scale * jax.random.normal(rng, shape, jnp.float32)
    if cuts:
        array = array * steps_of(rng, shape, cuts, -0.22, 0.18)
    return jnp.clip(array, -limit, limit).astype(dtype)


def setup_inputs(seed: int = 0, part: int = 0) -> dict:
    splits = jax.random.split(jax.random.key(seed), 6)
    own_keys = jax.random.split(jax.random.fold_in(splits[5], part), 6)
    pair_rep = centred(own_keys[0], (N, N, C), 1.0, 6.0, ((0, 16),))
    residue_mask = plant((jax.random.randint(own_keys[1], (N,), 0, 8) < 7).astype(jnp.int32), jax.random.fold_in(own_keys[1], 1), 0, 1)
    side_weights = centred(splits[2], (2, 5, C, C), C ** -0.5, 0.5)
    out_weights = centred(splits[3], (2, C, C), C ** -0.5, 0.5)
    norm_gains = jnp.clip(1.0 + 0.18 * jax.random.normal(splits[4], (2, 2, C), jnp.float32), 0.1, 1.9)
    return dict(pair_rep=pair_rep, residue_mask=residue_mask, side_weights=side_weights, out_weights=out_weights, norm_gains=norm_gains)


def layer_norm(values, gain):
    centered = values - lax.optimization_barrier(jnp.mean(values, axis=-1, keepdims=True))
    variance = lax.optimization_barrier(jnp.mean(centered * centered, axis=-1, keepdims=True))
    return centered * lax.rsqrt(variance + 1e-05) * gain

def linear_map(normed, weight):
    flat = normed.reshape(-1, normed.shape[-1])
    return jnp.dot(flat, weight, preferred_element_type=jnp.float32).reshape(normed.shape[:-1] + (weight.shape[1],))

def triangle_sums(left_proj, right_proj, incoming):
    size = left_proj.shape[0]
    width = left_proj.shape[2]
    left_t = jnp.moveaxis(left_proj, -1, 0).reshape(width // 16, 16, size, size)
    right_t = jnp.moveaxis(right_proj, -1, 0).reshape(width // 16, 16, size, size)

    def block_sum(pieces):
        left_b = pieces[0].astype(jnp.float32)
        right_b = pieces[1].astype(jnp.float32)
        if incoming:
            return jnp.einsum('cki,ckj->cij', left_b, right_b)
        return jnp.einsum('cik,cjk->cij', left_b, right_b)
    blocks = lax.map(block_sum, (left_t, right_t))
    return jnp.moveaxis(blocks.reshape(width, size, size), 0, -1)

def one_update(pair_now, residue_mask, weights, out_weight, gains, incoming):
    pair_f32 = pair_now.astype(jnp.float32)
    normed = layer_norm(pair_f32, gains[0]).astype(jnp.bfloat16)
    outs_list = [linear_map(normed, weights[index]) for index in range(5)]
    mask_f32 = residue_mask.astype(jnp.float32)
    pair_mask = (mask_f32[:, None] * mask_f32[None, :])[..., None]
    left_proj = (jax.nn.sigmoid(outs_list[0]) * outs_list[1] * pair_mask).astype(jnp.bfloat16)
    right_proj = (jax.nn.sigmoid(outs_list[2]) * outs_list[3] * pair_mask).astype(jnp.bfloat16)
    gate_vals = jax.nn.sigmoid(outs_list[4])
    triangle = triangle_sums(left_proj, right_proj, incoming)
    tri_normed = layer_norm(triangle, gains[1]).astype(jnp.bfloat16)
    projected = linear_map(tri_normed, out_weight)
    return (pair_f32 + gate_vals * projected).astype(jnp.bfloat16)

def reference(pair_rep, residue_mask, side_weights, out_weights, norm_gains):
    middle = one_update(pair_rep, residue_mask, side_weights[0], out_weights[0], norm_gains[0], False)
    return one_update(middle, residue_mask, side_weights[1], out_weights[1], norm_gains[1], True)
```

```python
import functools

import jax
import jax.numpy as jnp
from jax import lax
from jax.experimental import pallas as pl
from jax.experimental.pallas import tpu as pltpu
from jax.sharding import PartitionSpec as P

MESH = pl.DeviceIdType.MESH
CHUNK = 256
GROUP_BYTES = 1 << 20


def layer_norm(values, gain, axis):
    centered = values - jnp.mean(values, axis=axis, keepdims=True)
    variance = jnp.mean(centered * centered, axis=axis, keepdims=True)
    return centered * lax.rsqrt(variance + 1e-05) * gain


def one_side(normed, gate_weight, value_weight, pair_mask):
    both_weights = jnp.stack([gate_weight, value_weight])
    sides = jnp.einsum("rnd,qde->qern", normed, both_weights, preferred_element_type=jnp.float32)
    return (jax.nn.sigmoid(sides[0]) * sides[1] * pair_mask[None]).astype(jnp.bfloat16)


def send_sides(normed, weights, pair_mask):
    left_proj = one_side(normed, weights[0], weights[1], pair_mask)
    left_cols = lax.all_to_all(left_proj, "row", split_axis=0, concat_axis=1, tiled=True)
    right_proj = one_side(normed, weights[2], weights[3], pair_mask)
    right_cols = lax.all_to_all(right_proj, "row", split_axis=0, concat_axis=1, tiled=True)
    return (left_cols, right_cols)


def one_update(pair_now, pair_mask, weights, out_weight, gains, incoming):
    pair_f32 = pair_now.astype(jnp.float32)
    normed = layer_norm(pair_f32, gains[0], -1).astype(jnp.bfloat16)
    left_cols, right_cols = send_sides(normed, weights, pair_mask)
    gate_vals = jax.nn.sigmoid(
        jnp.einsum("rnd,de->rne", normed, weights[4], preferred_element_type=jnp.float32)
    )
    if incoming:
        triangle = jnp.einsum(
            "cki,ckj->cij", left_cols, right_cols, preferred_element_type=jnp.float32
        )
    else:
        triangle = jnp.einsum(
            "cik,cjk->cij", left_cols, right_cols, preferred_element_type=jnp.float32
        )
    own_rows = lax.all_to_all(
        triangle.astype(jnp.bfloat16), "row", split_axis=1, concat_axis=0, tiled=True
    ).astype(triangle.dtype)
    tri_normed = layer_norm(own_rows, gains[1][:, None, None], 0).astype(jnp.bfloat16)
    projected = jnp.einsum(
        "crn,ce->rne", tri_normed, out_weight, preferred_element_type=jnp.float32
    )
    return (pair_f32 + gate_vals * projected).astype(jnp.bfloat16)


def large_body(pair_rep, residue_mask, side_weights, out_weights, norm_gains):
    row_count = pair_rep.shape[0]
    first_row = lax.axis_index("row") * row_count
    mask_f32 = residue_mask.astype(jnp.float32)
    own_mask = lax.dynamic_slice_in_dim(mask_f32, first_row, row_count, 0)
    pair_mask = own_mask[:, None] * mask_f32[None, :]
    middle = one_update(pair_rep, pair_mask, side_weights[0], out_weights[0], norm_gains[0], False)
    return one_update(middle, pair_mask, side_weights[1], out_weights[1], norm_gains[1], True)


def sigmoid(values):
    return 0.5 * jnp.tanh(0.5 * values) + 0.5


def dot(a, b):
    return jnp.dot(a, b, preferred_element_type=jnp.float32)


def pair_kernel(
    ranks, size, rows,
    pair_ref, mask_ref, side_ref, out_ref, gain_ref, result_ref,
    pair_all, side_w, out_w, gain_w, mask_w, mask_col, pair_mask,
    left, right_t, gate, tri, pair_mid, normed_mid, right_mid,
    send_sem, recv_sem, load_sem,
):
    chan = pair_all.shape[1]
    block = rows * size
    grp, me = lax.axis_index("grp"), lax.axis_index("row")
    chips = ranks // 2
    sibling = me + 1 - 2 * (me % 2)
    peers = [(me + 2 * step) % ranks for step in range(1, chips)]

    barrier = pltpu.get_barrier_semaphore()
    for peer in peers + [sibling]:
        pl.semaphore_signal(barrier, inc=1, device_id=(grp, peer), device_id_type=MESH)

    def part(rank):
        return pair_all.at[pl.ds(pl.multiple_of(rank * block, block), block)]

    loads = [
        pltpu.make_async_copy(source, target, load_sem.at[index])
        for index, (source, target) in enumerate(
            [(pair_ref, part(me)), (mask_ref, mask_w), (side_ref, side_w), (out_ref, out_w), (gain_ref, gain_w)]
        )
    ]
    for load in loads:
        load.start()

    loads[1].wait()
    at_row = lax.broadcasted_iota(jnp.int32, (size, size), 0)
    at_col = lax.broadcasted_iota(jnp.int32, (size, size), 1)
    mask_row = jnp.broadcast_to(mask_w[...].astype(jnp.float32), (size, size))
    column = jnp.sum(jnp.where(at_row == at_col, mask_row, 0.0), axis=1, keepdims=True)
    mask_col[...] = jnp.broadcast_to(column, (size, chan))

    pl.semaphore_wait(barrier, chips)

    copies = []

    def put(source, rank, target):
        copy = pltpu.make_async_remote_copy(
            src_ref=source, dst_ref=part(rank), send_sem=send_sem.at[len(copies)],
            recv_sem=recv_sem.at[rank], device_id=(grp, target), device_id_type=MESH,
        )
        copy.start()
        copies.append(copy)

    def arrive(rank):
        pltpu.make_async_remote_copy(
            src_ref=part(rank), dst_ref=part(rank), send_sem=send_sem.at[0],
            recv_sem=recv_sem.at[rank], device_id=(grp, sibling), device_id_type=MESH,
        ).wait_recv()

    for peer in peers + [sibling]:
        put(pair_ref, me, peer)

    def fill_mask(first, carry):
        mask_one = mask_col[pl.ds(first, 1), :]
        pair_mask[pl.ds(pl.multiple_of(first * size, size), size), :] = mask_one * mask_col[...]
        return carry

    lax.fori_loop(0, size, fill_mask, 0)

    for peer in peers:
        arrive(peer)
        put(part(peer), peer, sibling)
    for load in (loads[0], loads[2], loads[3], loads[4]):
        load.wait()
    for step in range(chips):
        arrive((sibling + 2 * step) % ranks)

    gains = [[gain_w[u, pl.ds(q, 1), :] for q in range(2)] for u in range(2)]

    def project(step, carry):
        span = pl.ds(pl.multiple_of(step * CHUNK, CHUNK), CHUNK)
        normed = layer_norm(pair_all[span, :].astype(jnp.float32), gains[0][0], -1).astype(jnp.bfloat16)
        mask = pair_mask[span, :]
        lefts = dot(normed, jnp.concatenate([side_w[0, 0], side_w[0, 1]], axis=1))
        left[span, :] = (sigmoid(lefts[:, :chan]) * lefts[:, chan:] * mask).astype(jnp.bfloat16).astype(jnp.float32)
        rights = dot(normed, jnp.concatenate([side_w[0, 2], side_w[0, 3]], axis=1))
        right = (sigmoid(rights[:, :chan]) * rights[:, chan:] * mask).astype(jnp.bfloat16).astype(jnp.float32)
        for index in range(CHUNK // size):
            right_t[pl.ds(step * (CHUNK // size) + index, size, stride=size), :] = right[index * size:(index + 1) * size]
        gate[span, :] = sigmoid(dot(normed, side_w[0, 4]))
        return carry

    lax.fori_loop(0, size * size // CHUNK, project, 0)

    def outgoing(step, carry):
        first = pl.multiple_of(step * 4 * size, 4 * size)
        sums = [jnp.zeros((size, chan), jnp.float32) for _ in range(4)]
        for k in range(size):
            rights = right_t[k * size:(k + 1) * size, :]
            for index in range(4):
                sums[index] += left[pl.ds(first + index * size + k, 1), :] * rights
        for index in range(4):
            tri[pl.ds(pl.multiple_of(first + index * size, size), size), :] = sums[index]
        return carry

    lax.fori_loop(0, size // 4, outgoing, 0)

    def finish(step, carry):
        span = pl.ds(pl.multiple_of(step * CHUNK, CHUNK), CHUNK)
        tri_normed = layer_norm(tri[span, :], gains[0][1], -1).astype(jnp.bfloat16)
        middle = pair_all[span, :].astype(jnp.float32) + gate[span, :] * dot(tri_normed, out_w[0])
        middle = middle.astype(jnp.bfloat16).astype(jnp.float32)
        pair_mid[span, :] = middle
        normed = layer_norm(middle, gains[1][0], -1).astype(jnp.bfloat16)
        normed_mid[span, :] = normed.astype(jnp.float32)
        rights = dot(normed, jnp.concatenate([side_w[1, 2], side_w[1, 3]], axis=1))
        right = sigmoid(rights[:, :chan]) * rights[:, chan:] * pair_mask[span, :]
        right_mid[span, :] = right.astype(jnp.bfloat16).astype(jnp.float32)
        return carry

    lax.fori_loop(0, size * size // CHUNK, finish, 0)

    own = pl.ds(pl.multiple_of(me * block, block), block)
    columns = jnp.concatenate(
        [normed_mid[pl.ds(me * rows + index, size, stride=size), :] for index in range(rows)], axis=0
    ).astype(jnp.bfloat16)
    lefts = dot(columns, jnp.concatenate([side_w[1, 0], side_w[1, 1]], axis=1))
    left_own = sigmoid(lefts[:, :chan]) * lefts[:, chan:] * pair_mask[own, :]
    left_own = left_own.astype(jnp.bfloat16).astype(jnp.float32)
    gate_own = sigmoid(dot(normed_mid[own, :].astype(jnp.bfloat16), side_w[1, 4]))
    sums = [jnp.zeros((size, chan), jnp.float32) for _ in range(rows)]
    for k in range(size):
        rights = right_mid[k * size:(k + 1) * size, :]
        for index in range(rows):
            sums[index] += left_own[index * size + k:index * size + k + 1] * rights
    tri_normed = layer_norm(jnp.concatenate(sums, axis=0), gains[1][1], -1).astype(jnp.bfloat16)
    result_ref[...] = (pair_mid[own, :] + gate_own * dot(tri_normed, out_w[1])).astype(jnp.bfloat16)

    for copy in copies:
        copy.wait_send()


def group_body(ranks, pair_rep, residue_mask, side_weights, out_weights, norm_gains):
    rows, size, chan = pair_rep.shape
    pairs = size * size
    wide = pltpu.VMEM((pairs, chan), jnp.float32)
    result = pl.pallas_call(
        functools.partial(pair_kernel, ranks, size, rows),
        out_shape=jax.ShapeDtypeStruct((rows * size, chan), jnp.bfloat16),
        in_specs=[pl.BlockSpec(memory_space=pl.ANY)] * 5,
        out_specs=pl.BlockSpec(memory_space=pltpu.VMEM),
        scratch_shapes=[
            pltpu.VMEM((pairs, chan), jnp.bfloat16),
            pltpu.VMEM(side_weights.shape, jnp.bfloat16),
            pltpu.VMEM(out_weights.shape, jnp.bfloat16),
            pltpu.VMEM(norm_gains.shape, jnp.float32),
            pltpu.VMEM((1, size), jnp.int32),
            pltpu.VMEM((size, chan), jnp.float32),
            wide, wide, wide, wide, wide, wide, wide, wide,
            pltpu.SemaphoreType.DMA((ranks,)),
            pltpu.SemaphoreType.DMA((ranks,)),
            pltpu.SemaphoreType.DMA((5,)),
        ],
        compiler_params=pltpu.CompilerParams(
            collective_id=0, has_side_effects=True, vmem_limit_bytes=32 << 20
        ),
    )(pair_rep.reshape(rows * size, chan), residue_mask.reshape(1, size), side_weights, out_weights, norm_gains)
    return result.reshape(pair_rep.shape)


def body(ranks, pair_rep, residue_mask, side_weights, out_weights, norm_gains):
    rows, size, chan = pair_rep.shape
    fits = size * size * chan * 4 <= GROUP_BYTES and size * size % CHUNK == 0 and CHUNK % size == 0
    if fits and ranks % 2 == 0 and ranks > 2:
        return group_body(ranks, pair_rep, residue_mask, side_weights, out_weights, norm_gains)
    return large_body(pair_rep, residue_mask, side_weights, out_weights, norm_gains)


def solution(mesh):
    in_specs = (P(("grp", "row"), None, None), P("grp"), P(), P(), P())
    out_specs = P(("grp", "row"), None, None)
    mapped = functools.partial(body, mesh.shape["row"])
    return jax.shard_map(mapped, mesh=mesh, in_specs=in_specs, out_specs=out_specs, check_vma=False)
```

```python
import functools

import jax
import jax.numpy as jnp
from jax import lax
from jax.experimental import pallas as pl
from jax.experimental.pallas import tpu as pltpu
from jax.sharding import PartitionSpec as P

MESH = pl.DeviceIdType.MESH
CHUNK = 256
GROUP_BYTES = 1 << 20


def layer_norm(values, gain, axis):
    centered = values - jnp.mean(values, axis=axis, keepdims=True)
    variance = jnp.mean(centered * centered, axis=axis, keepdims=True)
    return centered * lax.rsqrt(variance + 1e-05) * gain


def one_side(normed, gate_weight, value_weight, pair_mask):
    both_weights = jnp.stack([gate_weight, value_weight])
    sides = jnp.einsum("rnd,qde->qern", normed, both_weights, preferred_element_type=jnp.float32)
    return (jax.nn.sigmoid(sides[0]) * sides[1] * pair_mask[None]).astype(jnp.bfloat16)


def send_sides(normed, weights, pair_mask):
    left_proj = one_side(normed, weights[0], weights[1], pair_mask)
    left_cols = lax.all_to_all(left_proj, "row", split_axis=0, concat_axis=1, tiled=True)
    right_proj = one_side(normed, weights[2], weights[3], pair_mask)
    right_cols = lax.all_to_all(right_proj, "row", split_axis=0, concat_axis=1, tiled=True)
    return (left_cols, right_cols)


def one_update(pair_now, pair_mask, weights, out_weight, gains, incoming):
    pair_f32 = pair_now.astype(jnp.float32)
    normed = layer_norm(pair_f32, gains[0], -1).astype(jnp.bfloat16)
    left_cols, right_cols = send_sides(normed, weights, pair_mask)
    gate_vals = jax.nn.sigmoid(
        jnp.einsum("rnd,de->rne", normed, weights[4], preferred_element_type=jnp.float32)
    )
    if incoming:
        triangle = jnp.einsum(
            "cki,ckj->cij", left_cols, right_cols, preferred_element_type=jnp.float32
        )
    else:
        triangle = jnp.einsum(
            "cik,cjk->cij", left_cols, right_cols, preferred_element_type=jnp.float32
        )
    own_rows = lax.all_to_all(
        triangle.astype(jnp.bfloat16), "row", split_axis=1, concat_axis=0, tiled=True
    ).astype(triangle.dtype)
    tri_normed = layer_norm(own_rows, gains[1][:, None, None], 0).astype(jnp.bfloat16)
    projected = jnp.einsum(
        "crn,ce->rne", tri_normed, out_weight, preferred_element_type=jnp.float32
    )
    return (pair_f32 + gate_vals * projected).astype(jnp.bfloat16)


def large_body(pair_rep, residue_mask, side_weights, out_weights, norm_gains):
    row_count = pair_rep.shape[0]
    first_row = lax.axis_index("row") * row_count
    mask_f32 = residue_mask.astype(jnp.float32)
    own_mask = lax.dynamic_slice_in_dim(mask_f32, first_row, row_count, 0)
    pair_mask = own_mask[:, None] * mask_f32[None, :]
    middle = one_update(pair_rep, pair_mask, side_weights[0], out_weights[0], norm_gains[0], False)
    return one_update(middle, pair_mask, side_weights[1], out_weights[1], norm_gains[1], True)


def sigmoid(values):
    return 0.5 * jnp.tanh(0.5 * values) + 0.5


def dot(a, b):
    return jnp.dot(a, b, preferred_element_type=jnp.float32)


def pair_kernel(
    ranks, size, rows,
    pair_ref, mask_ref, side_ref, out_ref, gain_ref, result_ref,
    pair_all, side_w, out_w, gain_w, mask_w, mask_col, pair_mask,
    left, right_t, gate, tri, pair_mid, normed_mid, right_mid,
    send_sem, recv_sem, load_sem,
):
    chan = pair_all.shape[1]
    block = rows * size
    grp, me = lax.axis_index("grp"), lax.axis_index("row")
    chips = ranks // 2
    sibling = me + 1 - 2 * (me % 2)
    peers = [(me + 2 * step) % ranks for step in range(1, chips)]

    barrier = pltpu.get_barrier_semaphore()
    for peer in peers + [sibling]:
        pl.semaphore_signal(barrier, inc=1, device_id=(grp, peer), device_id_type=MESH)

    def part(rank):
        return pair_all.at[pl.ds(pl.multiple_of(rank * block, block), block)]

    loads = [
        pltpu.make_async_copy(source, target, load_sem.at[index])
        for index, (source, target) in enumerate(
            [(pair_ref, part(me)), (mask_ref, mask_w), (side_ref, side_w), (out_ref, out_w), (gain_ref, gain_w)]
        )
    ]
    for load in loads:
        load.start()

    loads[1].wait()
    at_row = lax.broadcasted_iota(jnp.int32, (size, size), 0)
    at_col = lax.broadcasted_iota(jnp.int32, (size, size), 1)
    mask_row = jnp.broadcast_to(mask_w[...].astype(jnp.float32), (size, size))
    column = jnp.sum(jnp.where(at_row == at_col, mask_row, 0.0), axis=1, keepdims=True)
    mask_col[...] = jnp.broadcast_to(column, (size, chan))

    pl.semaphore_wait(barrier, chips)

    copies = []

    def put(source, rank, target):
        copy = pltpu.make_async_remote_copy(
            src_ref=source, dst_ref=part(rank), send_sem=send_sem.at[len(copies)],
            recv_sem=recv_sem.at[rank], device_id=(grp, target), device_id_type=MESH,
        )
        copy.start()
        copies.append(copy)

    def arrive(rank):
        pltpu.make_async_remote_copy(
            src_ref=part(rank), dst_ref=part(rank), send_sem=send_sem.at[0],
            recv_sem=recv_sem.at[rank], device_id=(grp, sibling), device_id_type=MESH,
        ).wait_recv()

    for peer in peers + [sibling]:
        put(pair_ref, me, peer)

    def fill_mask(first, carry):
        mask_one = mask_col[pl.ds(first, 1), :]
        pair_mask[pl.ds(pl.multiple_of(first * size, size), size), :] = mask_one * mask_col[...]
        return carry

    lax.fori_loop(0, size, fill_mask, 0)

    for peer in peers:
        arrive(peer)
        put(part(peer), peer, sibling)
    for load in (loads[0], loads[2], loads[3], loads[4]):
        load.wait()
    for step in range(chips):
        arrive((sibling + 2 * step) % ranks)

    gains = [[gain_w[u, pl.ds(q, 1), :] for q in range(2)] for u in range(2)]

    def project(step, carry):
        span = pl.ds(pl.multiple_of(step * CHUNK, CHUNK), CHUNK)
        normed = layer_norm(pair_all[span, :].astype(jnp.float32), gains[0][0], -1).astype(jnp.bfloat16)
        mask = pair_mask[span, :]
        lefts = dot(normed, jnp.concatenate([side_w[0, 0], side_w[0, 1]], axis=1))
        left[span, :] = (sigmoid(lefts[:, :chan]) * lefts[:, chan:] * mask).astype(jnp.bfloat16).astype(jnp.float32)
        rights = dot(normed, jnp.concatenate([side_w[0, 2], side_w[0, 3]], axis=1))
        right = (sigmoid(rights[:, :chan]) * rights[:, chan:] * mask).astype(jnp.bfloat16).astype(jnp.float32)
        for index in range(CHUNK // size):
            right_t[pl.ds(step * (CHUNK // size) + index, size, stride=size), :] = right[index * size:(index + 1) * size]
        gate[span, :] = sigmoid(dot(normed, side_w[0, 4]))
        return carry

    lax.fori_loop(0, size * size // CHUNK, project, 0)

    def outgoing(step, carry):
        first = pl.multiple_of(step * 4 * size, 4 * size)
        sums = [jnp.zeros((size, chan), jnp.float32) for _ in range(4)]
        for k in range(size):
            rights = right_t[k * size:(k + 1) * size, :]
            for index in range(4):
                sums[index] += left[pl.ds(first + index * size + k, 1), :] * rights
        for index in range(4):
            tri[pl.ds(pl.multiple_of(first + index * size, size), size), :] = sums[index]
        return carry

    lax.fori_loop(0, size // 4, outgoing, 0)

    def finish(step, carry):
        span = pl.ds(pl.multiple_of(step * CHUNK, CHUNK), CHUNK)
        tri_normed = layer_norm(tri[span, :], gains[0][1], -1).astype(jnp.bfloat16)
        middle = pair_all[span, :].astype(jnp.float32) + gate[span, :] * dot(tri_normed, out_w[0])
        middle = middle.astype(jnp.bfloat16).astype(jnp.float32)
        pair_mid[span, :] = middle
        normed = layer_norm(middle, gains[1][0], -1).astype(jnp.bfloat16)
        normed_mid[span, :] = normed.astype(jnp.float32)
        rights = dot(normed, jnp.concatenate([side_w[1, 2], side_w[1, 3]], axis=1))
        right = sigmoid(rights[:, :chan]) * rights[:, chan:] * pair_mask[span, :]
        right_mid[span, :] = right.astype(jnp.bfloat16).astype(jnp.float32)
        return carry

    lax.fori_loop(0, size * size // CHUNK, finish, 0)

    own = pl.ds(pl.multiple_of(me * block, block), block)
    columns = jnp.concatenate(
        [normed_mid[pl.ds(me * rows + index, size, stride=size), :] for index in range(rows)], axis=0
    ).astype(jnp.bfloat16)
    lefts = dot(columns, jnp.concatenate([side_w[1, 0], side_w[1, 1]], axis=1))
    left_own = sigmoid(lefts[:, :chan]) * lefts[:, chan:] * pair_mask[own, :]
    left_own = left_own.astype(jnp.bfloat16).astype(jnp.float32)
    gate_own = sigmoid(dot(normed_mid[own, :].astype(jnp.bfloat16), side_w[1, 4]))
    sums = [jnp.zeros((size, chan), jnp.float32) for _ in range(rows)]
    for k in range(size):
        rights = right_mid[k * size:(k + 1) * size, :]
        for index in range(rows):
            sums[index] += left_own[index * size + k:index * size + k + 1] * rights
    tri_normed = layer_norm(jnp.concatenate(sums, axis=0), gains[1][1], -1).astype(jnp.bfloat16)
    result_ref[...] = (pair_mid[own, :] + gate_own * dot(tri_normed, out_w[1])).astype(jnp.bfloat16)

    for copy in copies:
        copy.wait_send()


def group_body(ranks, pair_rep, residue_mask, side_weights, out_weights, norm_gains):
    rows, size, chan = pair_rep.shape
    pairs = size * size
    wide = pltpu.VMEM((pairs, chan), jnp.float32)
    result = pl.pallas_call(
        functools.partial(pair_kernel, ranks, size, rows),
        out_shape=jax.ShapeDtypeStruct((rows * size, chan), jnp.bfloat16),
        in_specs=[pl.BlockSpec(memory_space=pltpu.HBM)] * 5,
        out_specs=pl.BlockSpec(memory_space=pltpu.VMEM),
        scratch_shapes=[
            pltpu.VMEM((pairs, chan), jnp.bfloat16),
            pltpu.VMEM(side_weights.shape, jnp.bfloat16),
            pltpu.VMEM(out_weights.shape, jnp.bfloat16),
            pltpu.VMEM(norm_gains.shape, jnp.float32),
            pltpu.VMEM((1, size), jnp.int32),
            pltpu.VMEM((size, chan), jnp.float32),
            wide, wide, wide, wide, wide, wide, wide, wide,
            pltpu.SemaphoreType.DMA((ranks,)),
            pltpu.SemaphoreType.DMA((ranks,)),
            pltpu.SemaphoreType.DMA((5,)),
        ],
        compiler_params=pltpu.CompilerParams(
            collective_id=0, has_side_effects=True, vmem_limit_bytes=32 << 20
        ),
    )(pair_rep.reshape(rows * size, chan), residue_mask.reshape(1, size), side_weights, out_weights, norm_gains)
    return result.reshape(pair_rep.shape)


def body(ranks, pair_rep, residue_mask, side_weights, out_weights, norm_gains):
    rows, size, chan = pair_rep.shape
    fits = size * size * chan * 4 <= GROUP_BYTES and size * size % CHUNK == 0 and CHUNK % size == 0
    if fits and ranks % 2 == 0 and ranks > 2:
        return group_body(ranks, pair_rep, residue_mask, side_weights, out_weights, norm_gains)
    return large_body(pair_rep, residue_mask, side_weights, out_weights, norm_gains)


def solution(mesh):
    in_specs = (P(("grp", "row"), None, None), P("grp"), P(), P(), P())
    out_specs = P(("grp", "row"), None, None)
    mapped = functools.partial(body, mesh.shape["row"])
    return jax.shard_map(mapped, mesh=mesh, in_specs=in_specs, out_specs=out_specs, check_vma=False)
```

```python
import functools

import jax
import jax.numpy as jnp
from jax import lax
from jax.experimental import pallas as pl
from jax.experimental.pallas import tpu as pltpu
from jax.sharding import PartitionSpec as P

MESH = pl.DeviceIdType.MESH
CHUNK = 256
GROUP_BYTES = 1 << 20


def layer_norm(values, gain, axis):
    centered = values - jnp.mean(values, axis=axis, keepdims=True)
    variance = jnp.mean(centered * centered, axis=axis, keepdims=True)
    return centered * lax.rsqrt(variance + 1e-05) * gain


def one_side(normed, gate_weight, value_weight, pair_mask):
    both_weights = jnp.stack([gate_weight, value_weight])
    sides = jnp.einsum("rnd,qde->qern", normed, both_weights, preferred_element_type=jnp.float32)
    return (jax.nn.sigmoid(sides[0]) * sides[1] * pair_mask[None]).astype(jnp.bfloat16)


def send_sides(normed, weights, pair_mask):
    left_proj = one_side(normed, weights[0], weights[1], pair_mask)
    left_cols = lax.all_to_all(left_proj, "row", split_axis=0, concat_axis=1, tiled=True)
    right_proj = one_side(normed, weights[2], weights[3], pair_mask)
    right_cols = lax.all_to_all(right_proj, "row", split_axis=0, concat_axis=1, tiled=True)
    return (left_cols, right_cols)


def one_update(pair_now, pair_mask, weights, out_weight, gains, incoming):
    pair_f32 = pair_now.astype(jnp.float32)
    normed = layer_norm(pair_f32, gains[0], -1).astype(jnp.bfloat16)
    left_cols, right_cols = send_sides(normed, weights, pair_mask)
    gate_vals = jax.nn.sigmoid(
        jnp.einsum("rnd,de->rne", normed, weights[4], preferred_element_type=jnp.float32)
    )
    if incoming:
        triangle = jnp.einsum(
            "cki,ckj->cij", left_cols, right_cols, preferred_element_type=jnp.float32
        )
    else:
        triangle = jnp.einsum(
            "cik,cjk->cij", left_cols, right_cols, preferred_element_type=jnp.float32
        )
    own_rows = lax.all_to_all(
        triangle.astype(jnp.bfloat16), "row", split_axis=1, concat_axis=0, tiled=True
    ).astype(triangle.dtype)
    tri_normed = layer_norm(own_rows, gains[1][:, None, None], 0).astype(jnp.bfloat16)
    projected = jnp.einsum(
        "crn,ce->rne", tri_normed, out_weight, preferred_element_type=jnp.float32
    )
    return (pair_f32 + gate_vals * projected).astype(jnp.bfloat16)


def large_body(pair_rep, residue_mask, side_weights, out_weights, norm_gains):
    row_count = pair_rep.shape[0]
    first_row = lax.axis_index("row") * row_count
    mask_f32 = residue_mask.astype(jnp.float32)
    own_mask = lax.dynamic_slice_in_dim(mask_f32, first_row, row_count, 0)
    pair_mask = own_mask[:, None] * mask_f32[None, :]
    middle = one_update(pair_rep, pair_mask, side_weights[0], out_weights[0], norm_gains[0], False)
    return one_update(middle, pair_mask, side_weights[1], out_weights[1], norm_gains[1], True)


def sigmoid(values):
    return 0.5 * jnp.tanh(0.5 * values) + 0.5


def dot(a, b):
    return jnp.dot(a, b, preferred_element_type=jnp.float32)


def pair_kernel(
    ranks, size, rows,
    pair_ref, mask_ref, side_ref, out_ref, gain_ref, result_ref,
    pair_all, side_w, out_w, gain_w, mask_w, mask_col, pair_mask,
    left, right_t, gate, tri, pair_mid, normed_mid, right_mid,
    send_sem, recv_sem, load_sem,
):
    chan = pair_all.shape[1]
    block = rows * size
    grp, me = lax.axis_index("grp"), lax.axis_index("row")
    chips = ranks // 2
    sibling = me + 1 - 2 * (me % 2)
    peers = [(me + 2 * step) % ranks for step in range(1, chips)]

    barrier = pltpu.get_barrier_semaphore()
    for peer in peers + [sibling]:
        pl.semaphore_signal(barrier, inc=1, device_id=(grp, peer), device_id_type=MESH)

    def part(rank):
        return pair_all.at[pl.ds(pl.multiple_of(rank * block, block), block)]

    loads = [
        pltpu.make_async_copy(source, target, load_sem.at[index])
        for index, (source, target) in enumerate(
            [(pair_ref, part(me)), (mask_ref, mask_w), (side_ref, side_w), (out_ref, out_w), (gain_ref, gain_w)]
        )
    ]
    for load in loads:
        load.start()

    loads[1].wait()
    at_row = lax.broadcasted_iota(jnp.int32, (size, size), 0)
    at_col = lax.broadcasted_iota(jnp.int32, (size, size), 1)
    mask_row = jnp.broadcast_to(mask_w[...].astype(jnp.float32), (size, size))
    column = jnp.sum(jnp.where(at_row == at_col, mask_row, 0.0), axis=1, keepdims=True)
    mask_col[...] = jnp.broadcast_to(column, (size, chan))

    pl.semaphore_wait(barrier, chips)

    copies = []

    def put(source, rank, target):
        copy = pltpu.make_async_remote_copy(
            src_ref=source, dst_ref=part(rank), send_sem=send_sem.at[len(copies)],
            recv_sem=recv_sem.at[rank], device_id=(grp, target), device_id_type=MESH,
        )
        copy.start()
        copies.append(copy)

    def arrive(rank):
        pltpu.make_async_remote_copy(
            src_ref=part(rank), dst_ref=part(rank), send_sem=send_sem.at[0],
            recv_sem=recv_sem.at[rank], device_id=(grp, sibling), device_id_type=MESH,
        ).wait_recv()

    for peer in peers + [sibling]:
        put(pair_ref, me, peer)

    def fill_mask(first, carry):
        mask_one = mask_col[pl.ds(first, 1), :]
        pair_mask[pl.ds(pl.multiple_of(first * size, size), size), :] = mask_one * mask_col[...]
        return carry

    lax.fori_loop(0, size, fill_mask, 0)

    for peer in peers:
        arrive(peer)
        put(part(peer), peer, sibling)
    for load in (loads[0], loads[2], loads[3], loads[4]):
        load.wait()
    for step in range(chips):
        arrive((sibling + 2 * step) % ranks)

    gains = [[gain_w[u, pl.ds(q, 1), :] for q in range(2)] for u in range(2)]

    def project(step, carry):
        span = pl.ds(pl.multiple_of(step * CHUNK, CHUNK), CHUNK)
        normed = layer_norm(pair_all[span, :].astype(jnp.float32), gains[0][0], -1).astype(jnp.bfloat16)
        mask = pair_mask[span, :]
        lefts = dot(normed, jnp.concatenate([side_w[0, 0], side_w[0, 1]], axis=1))
        left[span, :] = (sigmoid(lefts[:, :chan]) * lefts[:, chan:] * mask).astype(jnp.bfloat16).astype(jnp.float32)
        rights = dot(normed, jnp.concatenate([side_w[0, 2], side_w[0, 3]], axis=1))
        right = (sigmoid(rights[:, :chan]) * rights[:, chan:] * mask).astype(jnp.bfloat16).astype(jnp.float32)
        for index in range(CHUNK // size):
            right_t[pl.ds(step * (CHUNK // size) + index, size, stride=size), :] = right[index * size:(index + 1) * size]
        gate[span, :] = sigmoid(dot(normed, side_w[0, 4]))
        return carry

    lax.fori_loop(0, size * size // CHUNK, project, 0)

    def outgoing(step, carry):
        first = pl.multiple_of(step * 4 * size, 4 * size)
        sums = [jnp.zeros((size, chan), jnp.float32) for _ in range(4)]
        for k in range(size):
            rights = right_t[k * size:(k + 1) * size, :]
            for index in range(4):
                sums[index] += left[pl.ds(first + index * size + k, 1), :] * rights
        for index in range(4):
            tri[pl.ds(pl.multiple_of(first + index * size, size), size), :] = sums[index]
        return carry

    lax.fori_loop(0, size // 4, outgoing, 0)

    def finish(step, carry):
        span = pl.ds(pl.multiple_of(step * CHUNK, CHUNK), CHUNK)
        tri_normed = layer_norm(tri[span, :], gains[0][1], -1).astype(jnp.bfloat16)
        middle = pair_all[span, :].astype(jnp.float32) + gate[span, :] * dot(tri_normed, out_w[0])
        middle = middle.astype(jnp.bfloat16).astype(jnp.float32)
        pair_mid[span, :] = middle
        normed = layer_norm(middle, gains[1][0], -1).astype(jnp.bfloat16)
        normed_mid[span, :] = normed.astype(jnp.float32)
        rights = dot(normed, jnp.concatenate([side_w[1, 2], side_w[1, 3]], axis=1))
        right = sigmoid(rights[:, :chan]) * rights[:, chan:] * pair_mask[span, :]
        right_mid[span, :] = right.astype(jnp.bfloat16).astype(jnp.float32)
        return carry

    lax.fori_loop(0, size * size // CHUNK, finish, 0)

    own = pl.ds(pl.multiple_of(me * block, block), block)
    columns = jnp.concatenate(
        [normed_mid[pl.ds(me * rows + index, size, stride=size), :] for index in range(rows)], axis=0
    ).astype(jnp.bfloat16)
    lefts = dot(columns, jnp.concatenate([side_w[1, 0], side_w[1, 1]], axis=1))
    left_own = sigmoid(lefts[:, :chan]) * lefts[:, chan:] * pair_mask[own, :]
    left_own = left_own.astype(jnp.bfloat16).astype(jnp.float32)
    gate_own = sigmoid(dot(normed_mid[own, :].astype(jnp.bfloat16), side_w[1, 4]))
    sums = [jnp.zeros((size, chan), jnp.float32) for _ in range(rows)]
    for k in range(size):
        rights = right_mid[k * size:(k + 1) * size, :]
        for index in range(rows):
            sums[index] += left_own[index * size + k:index * size + k + 1] * rights
    tri_normed = layer_norm(jnp.concatenate(sums, axis=0), gains[1][1], -1).astype(jnp.bfloat16)
    result_ref[...] = (pair_mid[own, :] + gate_own * dot(tri_normed, out_w[1])).astype(jnp.bfloat16)

    for copy in copies:
        copy.wait_send()


def group_body(ranks, pair_rep, residue_mask, side_weights, out_weights, norm_gains):
    rows, size, chan = pair_rep.shape
    pairs = size * size
    wide = pltpu.VMEM((pairs, chan), jnp.float32)
    result = pl.pallas_call(
        functools.partial(pair_kernel, ranks, size, rows),
        out_shape=pltpu.VMEM((rows * size, chan), jnp.bfloat16),
        in_specs=[pl.BlockSpec(memory_space=pltpu.HBM)] * 5,
        out_specs=pl.BlockSpec(memory_space=pltpu.VMEM),
        scratch_shapes=[
            pltpu.VMEM((pairs, chan), jnp.bfloat16),
            pltpu.VMEM(side_weights.shape, jnp.bfloat16),
            pltpu.VMEM(out_weights.shape, jnp.bfloat16),
            pltpu.VMEM(norm_gains.shape, jnp.float32),
            pltpu.VMEM((1, size), jnp.int32),
            pltpu.VMEM((size, chan), jnp.float32),
            wide, wide, wide, wide, wide, wide, wide, wide,
            pltpu.SemaphoreType.DMA((ranks,)),
            pltpu.SemaphoreType.DMA((ranks,)),
            pltpu.SemaphoreType.DMA((5,)),
        ],
        compiler_params=pltpu.CompilerParams(
            collective_id=0, has_side_effects=True, vmem_limit_bytes=60 << 20
        ),
    )(pair_rep.reshape(rows * size, chan), residue_mask.reshape(1, size), side_weights, out_weights, norm_gains)
    return result.reshape(pair_rep.shape)


def body(ranks, pair_rep, residue_mask, side_weights, out_weights, norm_gains):
    rows, size, chan = pair_rep.shape
    fits = size * size * chan * 4 <= GROUP_BYTES and size * size % CHUNK == 0 and CHUNK % size == 0
    if fits and ranks % 2 == 0 and ranks > 2:
        return group_body(ranks, pair_rep, residue_mask, side_weights, out_weights, norm_gains)
    return large_body(pair_rep, residue_mask, side_weights, out_weights, norm_gains)


def solution(mesh):
    in_specs = (P(("grp", "row"), None, None), P("grp"), P(), P(), P())
    out_specs = P(("grp", "row"), None, None)
    mapped = functools.partial(body, mesh.shape["row"])
    return jax.shard_map(mapped, mesh=mesh, in_specs=in_specs, out_specs=out_specs, check_vma=False)
```

```python
import functools

import jax
import jax.numpy as jnp
from jax import lax
from jax.experimental import pallas as pl
from jax.experimental.pallas import tpu as pltpu
from jax.sharding import PartitionSpec as P

MESH = pl.DeviceIdType.MESH
CHUNK = 512
WAVE = 2
MXU = False
UNROLL = 1
FOUR = 4
GROUP_BYTES = 1 << 20


def layer_norm(values, gain, axis):
    centered = values - jnp.mean(values, axis=axis, keepdims=True)
    variance = jnp.mean(centered * centered, axis=axis, keepdims=True)
    return centered * lax.rsqrt(variance + 1e-05) * gain


def one_side(normed, gate_weight, value_weight, pair_mask):
    both_weights = jnp.stack([gate_weight, value_weight])
    sides = jnp.einsum("rnd,qde->qern", normed, both_weights, preferred_element_type=jnp.float32)
    return (jax.nn.sigmoid(sides[0]) * sides[1] * pair_mask[None]).astype(jnp.bfloat16)


def send_sides(normed, weights, pair_mask):
    left_proj = one_side(normed, weights[0], weights[1], pair_mask)
    left_cols = lax.all_to_all(left_proj, "row", split_axis=0, concat_axis=1, tiled=True)
    right_proj = one_side(normed, weights[2], weights[3], pair_mask)
    right_cols = lax.all_to_all(right_proj, "row", split_axis=0, concat_axis=1, tiled=True)
    return (left_cols, right_cols)


def one_update(pair_now, pair_mask, weights, out_weight, gains, incoming):
    pair_f32 = pair_now.astype(jnp.float32)
    normed = layer_norm(pair_f32, gains[0], -1).astype(jnp.bfloat16)
    left_cols, right_cols = send_sides(normed, weights, pair_mask)
    gate_vals = jax.nn.sigmoid(
        jnp.einsum("rnd,de->rne", normed, weights[4], preferred_element_type=jnp.float32)
    )
    if incoming:
        triangle = jnp.einsum(
            "cki,ckj->cij", left_cols, right_cols, preferred_element_type=jnp.float32
        )
    else:
        triangle = jnp.einsum(
            "cik,cjk->cij", left_cols, right_cols, preferred_element_type=jnp.float32
        )
    own_rows = lax.all_to_all(
        triangle.astype(jnp.bfloat16), "row", split_axis=1, concat_axis=0, tiled=True
    ).astype(triangle.dtype)
    tri_normed = layer_norm(own_rows, gains[1][:, None, None], 0).astype(jnp.bfloat16)
    projected = jnp.einsum(
        "crn,ce->rne", tri_normed, out_weight, preferred_element_type=jnp.float32
    )
    return (pair_f32 + gate_vals * projected).astype(jnp.bfloat16)


def large_body(pair_rep, residue_mask, side_weights, out_weights, norm_gains):
    row_count = pair_rep.shape[0]
    first_row = lax.axis_index("row") * row_count
    mask_f32 = residue_mask.astype(jnp.float32)
    own_mask = lax.dynamic_slice_in_dim(mask_f32, first_row, row_count, 0)
    pair_mask = own_mask[:, None] * mask_f32[None, :]
    middle = one_update(pair_rep, pair_mask, side_weights[0], out_weights[0], norm_gains[0], False)
    return one_update(middle, pair_mask, side_weights[1], out_weights[1], norm_gains[1], True)


def waves(spans):
    return [list(range(begin, min(begin + WAVE, spans))) for begin in range(0, spans, WAVE)]


def mean_all(values, exact):
    chan = values.shape[1]
    high = values.astype(jnp.bfloat16)
    if exact:
        return dot(high, jnp.full((chan, chan), 1.0 / chan, jnp.bfloat16))
    low = (values - high.astype(jnp.float32)).astype(jnp.bfloat16)
    return dot(jnp.concatenate([high, low], axis=1), jnp.full((2 * chan, chan), 1.0 / chan, jnp.bfloat16))


def norm_rows(values, gain, exact):
    if not MXU:
        return layer_norm(values, gain, -1).astype(jnp.bfloat16)
    centered = values - mean_all(values, exact)
    variance = mean_all(centered * centered, False)
    return (centered * lax.rsqrt(variance + 1e-05) * gain).astype(jnp.bfloat16)


def sigmoid(values):
    return 0.5 * jnp.tanh(0.5 * values) + 0.5


def dot(a, b):
    return jnp.dot(a, b, preferred_element_type=jnp.float32)


def pair_kernel(
    ranks, size, rows,
    pair_ref, mask_ref, side_ref, out_ref, gain_ref, result_ref,
    pair_half, side_w, out_w, gain_w, mask_w, mask_col,
    right_put, right_got, mid_put, mid_got, left_put, left_got,
    pair_mask, left, gate, tri, pair_mid, normed_mid, right_mid, right_t,
    send_sem, recv_sem, pass_sem, take_sem, load_sem,
):
    chan = pair_half.shape[1]
    block = rows * size
    half = pair_half.shape[0]
    depth = half // size
    grp, me = lax.axis_index("grp"), lax.axis_index("row")
    spans = ranks // 4
    here, core = me // 4, me % 2
    slot, sibling = me // 2, me + 1 - 2 * (me % 2)
    beside = slot + 1 - 2 * (slot % 2)

    def slots_of(step):
        first = (here + step) % spans * 2
        return [first + slot % 2, first + beside % 2]

    direct = [slots_of(step) for step in range(spans)]
    direct[0] = direct[0][1:]
    peers = direct[0] + [peer for step in range(spans - 1, 0, -1) for peer in direct[step]]

    barrier = pltpu.get_barrier_semaphore()
    for rank in [2 * peer + core for peer in peers] + [sibling]:
        pl.semaphore_signal(barrier, inc=1, device_id=(grp, rank), device_id_type=MESH)

    def part(at):
        return pair_half.at[pl.ds(pl.multiple_of(at * block, block), block)]

    loads = [
        pltpu.make_async_copy(source, target, load_sem.at[index])
        for index, (source, target) in enumerate(
            [(pair_ref, part(slot)), (mask_ref, mask_w), (side_ref, side_w), (out_ref, out_w), (gain_ref, gain_w)]
        )
    ]
    for load in loads:
        load.start()

    loads[1].wait()
    at_row = lax.broadcasted_iota(jnp.int32, (size, size), 0)
    at_col = lax.broadcasted_iota(jnp.int32, (size, size), 1)
    mask_row = jnp.broadcast_to(mask_w[...].astype(jnp.float32), (size, size))
    column = jnp.sum(jnp.where(at_row == at_col, mask_row, 0.0), axis=1, keepdims=True)
    mask_col[...] = jnp.broadcast_to(column, (size, chan))

    pl.semaphore_wait(barrier, len(peers) + 1)

    copies = []
    for index, peer in enumerate(peers):
        copies.append(pltpu.make_async_remote_copy(
            src_ref=pair_ref, dst_ref=part(slot), send_sem=send_sem.at[index],
            recv_sem=recv_sem.at[slot], device_id=(grp, 2 * peer + core), device_id_type=MESH,
        ))
        copies[-1].start()

    def arrive(at):
        pltpu.make_async_remote_copy(
            src_ref=part(at), dst_ref=part(at), send_sem=send_sem.at[0],
            recv_sem=recv_sem.at[at], device_id=(grp, sibling), device_id_type=MESH,
        ).wait_recv()

    def swap(source, target, index):
        copy = pltpu.make_async_remote_copy(
            src_ref=source, dst_ref=target, send_sem=pass_sem.at[index],
            recv_sem=take_sem.at[index], device_id=(grp, sibling), device_id_type=MESH,
        )
        copy.start()
        copies.append(copy)
        return copy

    def fill_mask(at, carry):
        first = at // rows * 2 * rows + core * rows + at % rows
        mask_one = mask_col[pl.ds(first, 1), :]
        pair_mask[pl.ds(pl.multiple_of(at * size, size), size), :] = mask_one * mask_col[...]
        return carry

    lax.fori_loop(0, depth, fill_mask, 0)

    for load in (loads[0], loads[2], loads[3], loads[4]):
        load.wait()

    gains = [[gain_w[u, pl.ds(q, 1), :] for q in range(2)] for u in range(2)]
    chunk = 2 * block

    def spread(values, first, parity):
        for index in range(chunk // size):
            at = first // size // rows * 2 * rows + (index // rows * 2 + parity) * rows + index % rows
            right_t[pl.ds(at, size, stride=size), :] = values[index * size:(index + 1) * size]

    def project(firsts):
        values = jnp.concatenate([pair_half[pl.ds(first, chunk), :] for first in firsts], axis=0)
        normed = norm_rows(values.astype(jnp.float32), gains[0][0], True)
        mask = jnp.concatenate([pair_mask[pl.ds(first, chunk), :] for first in firsts], axis=0)
        rights = dot(normed, jnp.concatenate([side_w[0, 2], side_w[0, 3]], axis=1))
        rights = (sigmoid(rights[:, :chan]) * rights[:, chan:] * mask).astype(jnp.bfloat16)
        for at, first in enumerate(firsts):
            right_put[pl.ds(first, chunk), :] = rights[at * chunk:(at + 1) * chunk]
        rights = rights.astype(jnp.float32)
        lefts = dot(normed, jnp.concatenate([side_w[0, 0], side_w[0, 1]], axis=1))
        lefts = (sigmoid(lefts[:, :chan]) * lefts[:, chan:] * mask).astype(jnp.bfloat16).astype(jnp.float32)
        gates = sigmoid(dot(normed, side_w[0, 4]))
        for at, first in enumerate(firsts):
            rows_at = slice(at * chunk, (at + 1) * chunk)
            left[pl.ds(first, chunk), :] = lefts[rows_at]
            gate[pl.ds(first, chunk), :] = gates[rows_at]
            spread(rights[rows_at], first, core)

    swaps = []
    for steps in waves(spans):
        for step in steps:
            for at in direct[step]:
                arrive(at)
        firsts = [pl.multiple_of((here + step) % spans * chunk, chunk) for step in steps]
        project(firsts)
        for first, step in zip(firsts, steps):
            span = pl.ds(first, chunk)
            swaps.append(swap(right_put.at[span], right_got.at[span], step))
    for step in range(spans):
        swaps[step].wait_recv()
        first = pl.multiple_of((here + step) % spans * chunk, chunk)
        spread(right_got[pl.ds(first, chunk), :].astype(jnp.float32), first, 1 - core)

    def outgoing(step, carry):
        first = pl.multiple_of(step * 4 * size, 4 * size)
        sums = [jnp.zeros((size, chan), jnp.float32) for _ in range(4)]
        for k in range(size):
            rights = right_t[k * size:(k + 1) * size, :]
            for index in range(4):
                sums[index] += left[pl.ds(first + index * size + k, 1), :] * rights
        for index in range(4):
            tri[pl.ds(pl.multiple_of(first + index * size, size), size), :] = sums[index]
        return carry

    lax.fori_loop(0, depth // 4, outgoing, 0)

    swaps = []
    for begin in range(0, half, CHUNK):
        span = slice(begin, begin + CHUNK)
        tri_normed = norm_rows(tri[span, :], gains[0][1], False)
        middle = pair_half[span, :].astype(jnp.float32) + gate[span, :] * dot(tri_normed, out_w[0])
        middle = middle.astype(jnp.bfloat16).astype(jnp.float32)
        pair_mid[span, :] = middle
        normed = norm_rows(middle, gains[1][0], True)
        normed_mid[span, :] = normed.astype(jnp.float32)
        rights = dot(normed, jnp.concatenate([side_w[1, 2], side_w[1, 3]], axis=1))
        rights = (sigmoid(rights[:, :chan]) * rights[:, chan:] * pair_mask[span, :]).astype(jnp.bfloat16)
        mid_put[span, :] = rights
        swaps.append(swap(mid_put.at[span], mid_got.at[span], spans + begin // CHUNK))
        right_mid[span, :] = rights.astype(jnp.float32)

    wanted = [pl.ds(rank * rows + index, depth, stride=size) for rank in (sibling, me) for index in range(rows)]
    columns = jnp.concatenate([normed_mid[at, :] for at in wanted], axis=0).astype(jnp.bfloat16)
    column_mask = jnp.concatenate([pair_mask[at, :] for at in wanted], axis=0)
    lefts = dot(columns, jnp.concatenate([side_w[1, 0], side_w[1, 1]], axis=1))
    lefts = (sigmoid(lefts[:, :chan]) * lefts[:, chan:] * column_mask).astype(jnp.bfloat16)
    left_put[...] = lefts[:rows * depth]
    swaps.append(swap(left_put, left_got, spans + half // CHUNK))
    left_own = lefts[rows * depth:].astype(jnp.float32)

    own = pl.ds(pl.multiple_of(slot * block, block), block)
    gate_own = sigmoid(dot(normed_mid[own, :].astype(jnp.bfloat16), side_w[1, 4]))
    sums = [jnp.zeros((size, chan), jnp.float32) for _ in range(rows)]
    for k in range(depth):
        rights = right_mid[k * size:(k + 1) * size, :]
        for index in range(rows):
            sums[index] += left_own[index * depth + k:index * depth + k + 1] * rights
    for copy in swaps:
        copy.wait_recv()
    left_own = left_got[...].astype(jnp.float32)
    for k in range(depth):
        rights = mid_got[k * size:(k + 1) * size, :].astype(jnp.float32)
        for index in range(rows):
            sums[index] += left_own[index * depth + k:index * depth + k + 1] * rights
    tri_normed = norm_rows(jnp.concatenate(sums, axis=0), gains[1][1], False)
    result_ref[...] = (pair_mid[own, :] + gate_own * dot(tri_normed, out_w[1])).astype(jnp.bfloat16)

    for copy in copies:
        copy.wait_send()


def group_body(ranks, pair_rep, residue_mask, side_weights, out_weights, norm_gains):
    rows, size, chan = pair_rep.shape
    half = size * size // 2
    narrow, wide = pltpu.VMEM((half, chan), jnp.bfloat16), pltpu.VMEM((half, chan), jnp.float32)
    edge = pltpu.VMEM((rows * size // 2, chan), jnp.bfloat16)
    swaps = ranks // 4 + half // CHUNK + 1
    result = pl.pallas_call(
        functools.partial(pair_kernel, ranks, size, rows),
        out_shape=pltpu.VMEM((rows * size, chan), jnp.bfloat16),
        in_specs=[pl.BlockSpec(memory_space=pltpu.HBM)] * 5,
        out_specs=pl.BlockSpec(memory_space=pltpu.VMEM),
        scratch_shapes=[
            narrow,
            pltpu.VMEM(side_weights.shape, jnp.bfloat16),
            pltpu.VMEM(out_weights.shape, jnp.bfloat16),
            pltpu.VMEM(norm_gains.shape, jnp.float32),
            pltpu.VMEM((1, size), jnp.int32),
            pltpu.VMEM((size, chan), jnp.float32),
            narrow, narrow, narrow, narrow, edge, edge,
            wide, wide, wide, wide, wide, wide, wide,
            pltpu.VMEM((2 * half, chan), jnp.float32),
            pltpu.SemaphoreType.DMA((ranks // 2,)),
            pltpu.SemaphoreType.DMA((ranks // 2,)),
            pltpu.SemaphoreType.DMA((swaps,)),
            pltpu.SemaphoreType.DMA((swaps,)),
            pltpu.SemaphoreType.DMA((5,)),
        ],
        compiler_params=pltpu.CompilerParams(
            collective_id=0, has_side_effects=True, vmem_limit_bytes=60 << 20
        ),
    )(pair_rep.reshape(rows * size, chan), residue_mask.reshape(1, size), side_weights, out_weights, norm_gains)
    return result.reshape(pair_rep.shape)


def body(ranks, pair_rep, residue_mask, side_weights, out_weights, norm_gains):
    rows, size, chan = pair_rep.shape
    fits = size * size * chan * 4 <= GROUP_BYTES and size * size // 2 % CHUNK == 0 and rows * ranks == size and size % 16 == 0
    if fits and ranks % 4 == 0 and ranks > 4:
        return group_body(ranks, pair_rep, residue_mask, side_weights, out_weights, norm_gains)
    return large_body(pair_rep, residue_mask, side_weights, out_weights, norm_gains)


def solution(mesh):
    in_specs = (P(("grp", "row"), None, None), P("grp"), P(), P(), P())
    out_specs = P(("grp", "row"), None, None)
    mapped = functools.partial(body, mesh.shape["row"])
    return jax.shard_map(mapped, mesh=mesh, in_specs=in_specs, out_specs=out_specs, check_vma=False)
```

```python
import functools

import jax
import jax.numpy as jnp
from jax import lax
from jax.experimental import pallas as pl
from jax.experimental.pallas import tpu as pltpu
from jax.sharding import PartitionSpec as P

MESH = pl.DeviceIdType.MESH
CHUNK = 512
WAVE = 2
MXU = False
UNROLL = 1
FOUR = 4
GROUP_BYTES = 1 << 20


def layer_norm(values, gain, axis):
    centered = values - jnp.mean(values, axis=axis, keepdims=True)
    variance = jnp.mean(centered * centered, axis=axis, keepdims=True)
    return centered * lax.rsqrt(variance + 1e-05) * gain


def one_side(normed, gate_weight, value_weight, pair_mask):
    both_weights = jnp.stack([gate_weight, value_weight])
    sides = jnp.einsum("rnd,qde->qern", normed, both_weights, preferred_element_type=jnp.float32)
    return (jax.nn.sigmoid(sides[0]) * sides[1] * pair_mask[None]).astype(jnp.bfloat16)


def send_sides(normed, weights, pair_mask):
    left_proj = one_side(normed, weights[0], weights[1], pair_mask)
    left_cols = lax.all_to_all(left_proj, "row", split_axis=0, concat_axis=1, tiled=True)
    right_proj = one_side(normed, weights[2], weights[3], pair_mask)
    right_cols = lax.all_to_all(right_proj, "row", split_axis=0, concat_axis=1, tiled=True)
    return (left_cols, right_cols)


def one_update(pair_now, pair_mask, weights, out_weight, gains, incoming):
    pair_f32 = pair_now.astype(jnp.float32)
    normed = layer_norm(pair_f32, gains[0], -1).astype(jnp.bfloat16)
    left_cols, right_cols = send_sides(normed, weights, pair_mask)
    gate_vals = jax.nn.sigmoid(
        jnp.einsum("rnd,de->rne", normed, weights[4], preferred_element_type=jnp.float32)
    )
    if incoming:
        triangle = jnp.einsum(
            "cki,ckj->cij", left_cols, right_cols, preferred_element_type=jnp.float32
        )
    else:
        triangle = jnp.einsum(
            "cik,cjk->cij", left_cols, right_cols, preferred_element_type=jnp.float32
        )
    own_rows = lax.all_to_all(
        triangle.astype(jnp.bfloat16), "row", split_axis=1, concat_axis=0, tiled=True
    ).astype(triangle.dtype)
    tri_normed = layer_norm(own_rows, gains[1][:, None, None], 0).astype(jnp.bfloat16)
    projected = jnp.einsum(
        "crn,ce->rne", tri_normed, out_weight, preferred_element_type=jnp.float32
    )
    return (pair_f32 + gate_vals * projected).astype(jnp.bfloat16)


def large_body(pair_rep, residue_mask, side_weights, out_weights, norm_gains):
    row_count = pair_rep.shape[0]
    first_row = lax.axis_index("row") * row_count
    mask_f32 = residue_mask.astype(jnp.float32)
    own_mask = lax.dynamic_slice_in_dim(mask_f32, first_row, row_count, 0)
    pair_mask = own_mask[:, None] * mask_f32[None, :]
    middle = one_update(pair_rep, pair_mask, side_weights[0], out_weights[0], norm_gains[0], False)
    return one_update(middle, pair_mask, side_weights[1], out_weights[1], norm_gains[1], True)


def waves(spans):
    return [list(range(begin, min(begin + WAVE, spans))) for begin in range(0, spans, WAVE)]


def mean_all(values, exact):
    chan = values.shape[1]
    high = values.astype(jnp.bfloat16)
    if exact:
        return dot(high, jnp.full((chan, chan), 1.0 / chan, jnp.bfloat16))
    low = (values - high.astype(jnp.float32)).astype(jnp.bfloat16)
    return dot(jnp.concatenate([high, low], axis=1), jnp.full((2 * chan, chan), 1.0 / chan, jnp.bfloat16))


def norm_rows(values, gain, exact):
    if not MXU:
        return layer_norm(values, gain, -1).astype(jnp.bfloat16)
    centered = values - mean_all(values, exact)
    variance = mean_all(centered * centered, False)
    return (centered * lax.rsqrt(variance + 1e-05) * gain).astype(jnp.bfloat16)


def sigmoid(values):
    return 0.5 * jnp.tanh(0.5 * values) + 0.5


def dot(a, b):
    return jnp.dot(a, b, preferred_element_type=jnp.float32)


def pair_kernel(
    ranks, size, rows,
    pair_ref, mask_ref, side_ref, out_ref, gain_ref, result_ref,
    pair_half, side_w, out_w, gain_w, mask_w, mask_col,
    right_put, right_got, mid_put, mid_got, left_put, left_got,
    pair_mask, left, gate, tri, pair_mid, normed_mid, right_mid, right_t,
    send_sem, recv_sem, pass_sem, take_sem, load_sem,
):
    chan = pair_half.shape[1]
    block = rows * size
    half = pair_half.shape[0]
    depth = half // size
    grp, me = lax.axis_index("grp"), lax.axis_index("row")
    spans = ranks // 4
    here, core = me // 4, me % 2
    slot, sibling = me // 2, me + 1 - 2 * (me % 2)
    beside = slot + 1 - 2 * (slot % 2)

    def slots_of(step):
        first = (here + step) % spans * 2
        return [first + slot % 2, first + beside % 2]

    direct = [slots_of(step) for step in range(spans)]
    direct[0] = direct[0][1:]
    peers = direct[0] + [peer for step in range(spans - 1, 0, -1) for peer in direct[step]]

    barrier = pltpu.get_barrier_semaphore()
    for rank in [2 * peer + core for peer in peers] + [sibling]:
        pl.semaphore_signal(barrier, inc=1, device_id=(grp, rank), device_id_type=MESH)

    def part(at):
        return pair_half.at[pl.ds(pl.multiple_of(at * block, block), block)]

    loads = [
        pltpu.make_async_copy(source, target, load_sem.at[index])
        for index, (source, target) in enumerate(
            [(pair_ref, part(slot)), (mask_ref, mask_w), (side_ref, side_w), (out_ref, out_w), (gain_ref, gain_w)]
        )
    ]
    for load in loads:
        load.start()

    loads[1].wait()
    at_row = lax.broadcasted_iota(jnp.int32, (size, size), 0)
    at_col = lax.broadcasted_iota(jnp.int32, (size, size), 1)
    mask_row = jnp.broadcast_to(mask_w[...].astype(jnp.float32), (size, size))
    column = jnp.sum(jnp.where(at_row == at_col, mask_row, 0.0), axis=1, keepdims=True)
    mask_col[...] = jnp.broadcast_to(column, (size, chan))

    loads[0].wait()
    pl.semaphore_wait(barrier, len(peers) + 1)

    copies = []
    for index, peer in enumerate(peers):
        copies.append(pltpu.make_async_remote_copy(
            src_ref=part(slot), dst_ref=part(slot), send_sem=send_sem.at[index],
            recv_sem=recv_sem.at[slot], device_id=(grp, 2 * peer + core), device_id_type=MESH,
        ))
        copies[-1].start()

    def arrive(at):
        pltpu.make_async_remote_copy(
            src_ref=part(at), dst_ref=part(at), send_sem=send_sem.at[0],
            recv_sem=recv_sem.at[at], device_id=(grp, sibling), device_id_type=MESH,
        ).wait_recv()

    def swap(source, target, index):
        copy = pltpu.make_async_remote_copy(
            src_ref=source, dst_ref=target, send_sem=pass_sem.at[index],
            recv_sem=take_sem.at[index], device_id=(grp, sibling), device_id_type=MESH,
        )
        copy.start()
        copies.append(copy)
        return copy

    def fill_mask(at, carry):
        first = at // rows * 2 * rows + core * rows + at % rows
        mask_one = mask_col[pl.ds(first, 1), :]
        pair_mask[pl.ds(pl.multiple_of(at * size, size), size), :] = mask_one * mask_col[...]
        return carry

    lax.fori_loop(0, depth, fill_mask, 0)

    for load in loads[2:]:
        load.wait()

    gains = [[gain_w[u, pl.ds(q, 1), :] for q in range(2)] for u in range(2)]
    chunk = 2 * block

    def spread(values, first, turn):
        for index in range(chunk // size):
            at = turn * depth + index % rows * (ranks // 2) + first // block + index // rows
            right_t[pl.ds(at, size, stride=size), :] = values[index * size:(index + 1) * size]

    def project(firsts):
        values = jnp.concatenate([pair_half[pl.ds(first, chunk), :] for first in firsts], axis=0)
        normed = norm_rows(values.astype(jnp.float32), gains[0][0], True)
        mask = jnp.concatenate([pair_mask[pl.ds(first, chunk), :] for first in firsts], axis=0)
        rights = dot(normed, jnp.concatenate([side_w[0, 2], side_w[0, 3]], axis=1))
        rights = (sigmoid(rights[:, :chan]) * rights[:, chan:] * mask).astype(jnp.bfloat16)
        for at, first in enumerate(firsts):
            right_put[pl.ds(first, chunk), :] = rights[at * chunk:(at + 1) * chunk]
        rights = rights.astype(jnp.float32)
        lefts = dot(normed, jnp.concatenate([side_w[0, 0], side_w[0, 1]], axis=1))
        lefts = (sigmoid(lefts[:, :chan]) * lefts[:, chan:] * mask).astype(jnp.bfloat16).astype(jnp.float32)
        gates = sigmoid(dot(normed, side_w[0, 4]))
        for at, first in enumerate(firsts):
            rows_at = slice(at * chunk, (at + 1) * chunk)
            left[pl.ds(first, chunk), :] = lefts[rows_at]
            gate[pl.ds(first, chunk), :] = gates[rows_at]
            spread(rights[rows_at], first, 0)

    swaps = []
    for steps in waves(spans):
        for step in steps:
            for at in direct[step]:
                arrive(at)
        firsts = [pl.multiple_of((here + step) % spans * chunk, chunk) for step in steps]
        project(firsts)
        for first, step in zip(firsts, steps):
            span = pl.ds(first, chunk)
            swaps.append(swap(right_put.at[span], right_got.at[span], step))
    def outgoing(turn, step, carry):
        first = pl.multiple_of(step * 8 * size, 8 * size)
        sums = [jnp.zeros((depth, chan), jnp.float32) for _ in range(8)]
        for k in range(size):
            rights = right_t[k * size + turn * depth:k * size + (turn + 1) * depth, :]
            for index in range(8):
                sums[index] += left[pl.ds(first + index * size + k, 1), :] * rights
        lead = core * rows if turn == 0 else (1 - core) * rows
        count = ranks // 2
        for index in range(8):
            for row in range(rows):
                at = first + index * size + lead + row
                tri[pl.ds(at, count, stride=2 * rows), :] = sums[index][row * count:(row + 1) * count]
        return carry

    lax.fori_loop(0, depth // 8, functools.partial(outgoing, 0), 0, unroll=True)
    for step in range(spans):
        swaps[step].wait_recv()
        first = pl.multiple_of((here + step) % spans * chunk, chunk)
        spread(right_got[pl.ds(first, chunk), :].astype(jnp.float32), first, 1)
    lax.fori_loop(0, depth // 8, functools.partial(outgoing, 1), 0, unroll=True)

    swaps = []
    for begin in range(0, half, CHUNK):
        span = slice(begin, begin + CHUNK)
        tri_normed = norm_rows(tri[span, :], gains[0][1], False)
        middle = pair_half[span, :].astype(jnp.float32) + gate[span, :] * dot(tri_normed, out_w[0])
        middle = middle.astype(jnp.bfloat16).astype(jnp.float32)
        pair_mid[span, :] = middle
        normed = norm_rows(middle, gains[1][0], True)
        normed_mid[span, :] = normed.astype(jnp.float32)
        rights = dot(normed, jnp.concatenate([side_w[1, 2], side_w[1, 3]], axis=1))
        rights = (sigmoid(rights[:, :chan]) * rights[:, chan:] * pair_mask[span, :]).astype(jnp.bfloat16)
        mid_put[span, :] = rights
        swaps.append(swap(mid_put.at[span], mid_got.at[span], spans + begin // CHUNK))
        right_mid[span, :] = rights.astype(jnp.float32)

    wanted = [pl.ds(rank * rows + index, depth, stride=size) for rank in (sibling, me) for index in range(rows)]
    columns = jnp.concatenate([normed_mid[at, :] for at in wanted], axis=0).astype(jnp.bfloat16)
    column_mask = jnp.concatenate([pair_mask[at, :] for at in wanted], axis=0)
    lefts = dot(columns, jnp.concatenate([side_w[1, 0], side_w[1, 1]], axis=1))
    lefts = (sigmoid(lefts[:, :chan]) * lefts[:, chan:] * column_mask).astype(jnp.bfloat16)
    left_put[...] = lefts[:rows * depth]
    swaps.append(swap(left_put, left_got, spans + half // CHUNK))
    left_own = lefts[rows * depth:].astype(jnp.float32)

    own = pl.ds(pl.multiple_of(slot * block, block), block)
    gate_own = sigmoid(dot(normed_mid[own, :].astype(jnp.bfloat16), side_w[1, 4]))
    sums = [jnp.zeros((size, chan), jnp.float32) for _ in range(rows)]
    for k in range(depth):
        rights = right_mid[k * size:(k + 1) * size, :]
        for index in range(rows):
            sums[index] += left_own[index * depth + k:index * depth + k + 1] * rights
    for copy in swaps:
        copy.wait_recv()
    left_own = left_got[...].astype(jnp.float32)
    for k in range(depth):
        rights = mid_got[k * size:(k + 1) * size, :].astype(jnp.float32)
        for index in range(rows):
            sums[index] += left_own[index * depth + k:index * depth + k + 1] * rights
    tri_normed = norm_rows(jnp.concatenate(sums, axis=0), gains[1][1], False)
    result_ref[...] = (pair_mid[own, :] + gate_own * dot(tri_normed, out_w[1])).astype(jnp.bfloat16)

    for copy in copies:
        copy.wait_send()


def group_body(ranks, pair_rep, residue_mask, side_weights, out_weights, norm_gains):
    rows, size, chan = pair_rep.shape
    half = size * size // 2
    narrow, wide = pltpu.VMEM((half, chan), jnp.bfloat16), pltpu.VMEM((half, chan), jnp.float32)
    edge = pltpu.VMEM((rows * size // 2, chan), jnp.bfloat16)
    swaps = ranks // 4 + half // CHUNK + 1
    result = pl.pallas_call(
        functools.partial(pair_kernel, ranks, size, rows),
        out_shape=pltpu.VMEM((rows * size, chan), jnp.bfloat16),
        in_specs=[pl.BlockSpec(memory_space=pltpu.HBM)] * 5,
        out_specs=pl.BlockSpec(memory_space=pltpu.VMEM),
        scratch_shapes=[
            narrow,
            pltpu.VMEM(side_weights.shape, jnp.bfloat16),
            pltpu.VMEM(out_weights.shape, jnp.bfloat16),
            pltpu.VMEM(norm_gains.shape, jnp.float32),
            pltpu.VMEM((1, size), jnp.int32),
            pltpu.VMEM((size, chan), jnp.float32),
            narrow, narrow, narrow, narrow, edge, edge,
            wide, wide, wide, wide, wide, wide, wide,
            pltpu.VMEM((2 * half, chan), jnp.float32),
            pltpu.SemaphoreType.DMA((ranks // 2,)),
            pltpu.SemaphoreType.DMA((ranks // 2,)),
            pltpu.SemaphoreType.DMA((swaps,)),
            pltpu.SemaphoreType.DMA((swaps,)),
            pltpu.SemaphoreType.DMA((5,)),
        ],
        compiler_params=pltpu.CompilerParams(
            collective_id=0, has_side_effects=True, vmem_limit_bytes=60 << 20
        ),
    )(pair_rep.reshape(rows * size, chan), residue_mask.reshape(1, size), side_weights, out_weights, norm_gains)
    return result.reshape(pair_rep.shape)


def body(ranks, pair_rep, residue_mask, side_weights, out_weights, norm_gains):
    rows, size, chan = pair_rep.shape
    fits = size * size * chan * 4 <= GROUP_BYTES and size * size // 2 % CHUNK == 0 and rows * ranks == size and size % 16 == 0
    if fits and ranks % 4 == 0 and ranks > 4:
        return group_body(ranks, pair_rep, residue_mask, side_weights, out_weights, norm_gains)
    return large_body(pair_rep, residue_mask, side_weights, out_weights, norm_gains)


def solution(mesh):
    in_specs = (P(("grp", "row"), None, None), P("grp"), P(), P(), P())
    out_specs = P(("grp", "row"), None, None)
    mapped = functools.partial(body, mesh.shape["row"])
    return jax.shard_map(mapped, mesh=mesh, in_specs=in_specs, out_specs=out_specs, check_vma=False)
```

```python
import functools

import jax
import jax.numpy as jnp
from jax import lax
from jax.experimental import pallas as pl
from jax.experimental.pallas import tpu as pltpu
from jax.sharding import PartitionSpec as P

MESH = pl.DeviceIdType.MESH
CHUNK = 512
WAVE = 2
MXU = False
GROUP_BYTES = 1 << 20


def layer_norm(values, gain, axis):
    centered = values - jnp.mean(values, axis=axis, keepdims=True)
    variance = jnp.mean(centered * centered, axis=axis, keepdims=True)
    return centered * lax.rsqrt(variance + 1e-05) * gain


def one_side(normed, gate_weight, value_weight, pair_mask):
    both_weights = jnp.stack([gate_weight, value_weight])
    sides = jnp.einsum("rnd,qde->qern", normed, both_weights, preferred_element_type=jnp.float32)
    return (jax.nn.sigmoid(sides[0]) * sides[1] * pair_mask[None]).astype(jnp.bfloat16)


def send_sides(normed, weights, pair_mask):
    left_proj = one_side(normed, weights[0], weights[1], pair_mask)
    left_cols = lax.all_to_all(left_proj, "row", split_axis=0, concat_axis=1, tiled=True)
    right_proj = one_side(normed, weights[2], weights[3], pair_mask)
    right_cols = lax.all_to_all(right_proj, "row", split_axis=0, concat_axis=1, tiled=True)
    return (left_cols, right_cols)


def one_update(pair_now, pair_mask, weights, out_weight, gains, incoming):
    pair_f32 = pair_now.astype(jnp.float32)
    normed = layer_norm(pair_f32, gains[0], -1).astype(jnp.bfloat16)
    left_cols, right_cols = send_sides(normed, weights, pair_mask)
    gate_vals = jax.nn.sigmoid(
        jnp.einsum("rnd,de->rne", normed, weights[4], preferred_element_type=jnp.float32)
    )
    if incoming:
        triangle = jnp.einsum(
            "cki,ckj->cij", left_cols, right_cols, preferred_element_type=jnp.float32
        )
    else:
        triangle = jnp.einsum(
            "cik,cjk->cij", left_cols, right_cols, preferred_element_type=jnp.float32
        )
    own_rows = lax.all_to_all(
        triangle.astype(jnp.bfloat16), "row", split_axis=1, concat_axis=0, tiled=True
    ).astype(triangle.dtype)
    tri_normed = layer_norm(own_rows, gains[1][:, None, None], 0).astype(jnp.bfloat16)
    projected = jnp.einsum(
        "crn,ce->rne", tri_normed, out_weight, preferred_element_type=jnp.float32
    )
    return (pair_f32 + gate_vals * projected).astype(jnp.bfloat16)


def large_body(pair_rep, residue_mask, side_weights, out_weights, norm_gains):
    row_count = pair_rep.shape[0]
    first_row = lax.axis_index("row") * row_count
    mask_f32 = residue_mask.astype(jnp.float32)
    own_mask = lax.dynamic_slice_in_dim(mask_f32, first_row, row_count, 0)
    pair_mask = own_mask[:, None] * mask_f32[None, :]
    middle = one_update(pair_rep, pair_mask, side_weights[0], out_weights[0], norm_gains[0], False)
    return one_update(middle, pair_mask, side_weights[1], out_weights[1], norm_gains[1], True)


def waves(spans):
    return [list(range(begin, min(begin + WAVE, spans))) for begin in range(0, spans, WAVE)]


def mean_all(values, exact):
    chan = values.shape[1]
    high = values.astype(jnp.bfloat16)
    if exact:
        return dot(high, jnp.full((chan, chan), 1.0 / chan, jnp.bfloat16))
    low = (values - high.astype(jnp.float32)).astype(jnp.bfloat16)
    return dot(jnp.concatenate([high, low], axis=1), jnp.full((2 * chan, chan), 1.0 / chan, jnp.bfloat16))


def norm_rows(values, gain, exact):
    if not MXU:
        return layer_norm(values, gain, -1).astype(jnp.bfloat16)
    centered = values - mean_all(values, exact)
    variance = mean_all(centered * centered, False)
    return (centered * lax.rsqrt(variance + 1e-05) * gain).astype(jnp.bfloat16)


def sigmoid(values):
    return 0.5 * jnp.tanh(0.5 * values) + 0.5


def dot(a, b):
    return jnp.dot(a, b, preferred_element_type=jnp.float32)


def pair_kernel(
    ranks, size, rows,
    pair_ref, mask_ref, side_ref, out_ref, gain_ref, result_ref,
    pair_half, side_w, out_w, gain_w, mask_w, mask_col,
    right_put, right_got, mid_put, mid_got, left_put, left_got,
    pair_mask, left, gate, tri, pair_mid, normed_mid, right_mid, right_t,
    send_sem, recv_sem, pass_sem, take_sem, load_sem,
):
    chan = pair_half.shape[1]
    block = rows * size
    half = pair_half.shape[0]
    depth = half // size
    grp, me = lax.axis_index("grp"), lax.axis_index("row")
    spans = ranks // 4
    here, core = me // 4, me % 2
    slot, sibling = me // 2, me + 1 - 2 * (me % 2)
    beside = slot + 1 - 2 * (slot % 2)

    def slots_of(step):
        first = (here + step) % spans * 2
        return [first + slot % 2, first + beside % 2]

    direct = [slots_of(step) for step in range(spans)]
    direct[0] = direct[0][1:]
    peers = direct[0] + [peer for step in range(1, spans) for peer in direct[step]]

    barrier = pltpu.get_barrier_semaphore()
    for rank in [2 * peer + core for peer in peers] + [sibling]:
        pl.semaphore_signal(barrier, inc=1, device_id=(grp, rank), device_id_type=MESH)

    def part(at):
        return pair_half.at[pl.ds(pl.multiple_of(at * block, block), block)]

    loads = [
        pltpu.make_async_copy(source, target, load_sem.at[index])
        for index, (source, target) in enumerate(
            [(pair_ref, part(slot)), (mask_ref, mask_w), (side_ref, side_w), (out_ref, out_w), (gain_ref, gain_w)]
        )
    ]
    for load in loads:
        load.start()

    loads[1].wait()
    at_row = lax.broadcasted_iota(jnp.int32, (size, size), 0)
    at_col = lax.broadcasted_iota(jnp.int32, (size, size), 1)
    mask_row = jnp.broadcast_to(mask_w[...].astype(jnp.float32), (size, size))
    column = jnp.sum(jnp.where(at_row == at_col, mask_row, 0.0), axis=1, keepdims=True)
    mask_col[...] = jnp.broadcast_to(column, (size, chan))

    loads[0].wait()
    pl.semaphore_wait(barrier, len(peers) + 1)

    copies = []
    for index, peer in enumerate(peers):
        copies.append(pltpu.make_async_remote_copy(
            src_ref=part(slot), dst_ref=part(slot), send_sem=send_sem.at[index],
            recv_sem=recv_sem.at[slot], device_id=(grp, 2 * peer + core), device_id_type=MESH,
        ))
        copies[-1].start()

    def arrive(at):
        pltpu.make_async_remote_copy(
            src_ref=part(at), dst_ref=part(at), send_sem=send_sem.at[0],
            recv_sem=recv_sem.at[at], device_id=(grp, sibling), device_id_type=MESH,
        ).wait_recv()

    def swap(source, target, index):
        copy = pltpu.make_async_remote_copy(
            src_ref=source, dst_ref=target, send_sem=pass_sem.at[index],
            recv_sem=take_sem.at[index], device_id=(grp, sibling), device_id_type=MESH,
        )
        copy.start()
        copies.append(copy)
        return copy

    def fill_mask(at, carry):
        first = at // rows * 2 * rows + core * rows + at % rows
        mask_one = mask_col[pl.ds(first, 1), :]
        pair_mask[pl.ds(pl.multiple_of(at * size, size), size), :] = mask_one * mask_col[...]
        return carry

    lax.fori_loop(0, depth, fill_mask, 0)

    for load in loads[2:]:
        load.wait()

    gains = [[gain_w[u, pl.ds(q, 1), :] for q in range(2)] for u in range(2)]
    chunk = 2 * block

    def spread(values, first, turn):
        for index in range(chunk // size):
            at = turn * depth + index % rows * (ranks // 2) + first // block + index // rows
            right_t[pl.ds(at, size, stride=size), :] = values[index * size:(index + 1) * size]

    def project(firsts):
        values = jnp.concatenate([pair_half[pl.ds(first, chunk), :] for first in firsts], axis=0)
        normed = norm_rows(values.astype(jnp.float32), gains[0][0], True)
        mask = jnp.concatenate([pair_mask[pl.ds(first, chunk), :] for first in firsts], axis=0)
        rights = dot(normed, jnp.concatenate([side_w[0, 2], side_w[0, 3]], axis=1))
        rights = (sigmoid(rights[:, :chan]) * rights[:, chan:] * mask).astype(jnp.bfloat16)
        for at, first in enumerate(firsts):
            right_put[pl.ds(first, chunk), :] = rights[at * chunk:(at + 1) * chunk]
        rights = rights.astype(jnp.float32)
        lefts = dot(normed, jnp.concatenate([side_w[0, 0], side_w[0, 1]], axis=1))
        lefts = (sigmoid(lefts[:, :chan]) * lefts[:, chan:] * mask).astype(jnp.bfloat16).astype(jnp.float32)
        gates = sigmoid(dot(normed, side_w[0, 4]))
        for at, first in enumerate(firsts):
            rows_at = slice(at * chunk, (at + 1) * chunk)
            left[pl.ds(first, chunk), :] = lefts[rows_at]
            gate[pl.ds(first, chunk), :] = gates[rows_at]
            spread(rights[rows_at], first, 0)

    swaps = []
    for steps in waves(spans):
        for step in steps:
            for at in direct[step]:
                arrive(at)
        firsts = [pl.multiple_of((here + step) % spans * chunk, chunk) for step in steps]
        project(firsts)
        for first, step in zip(firsts, steps):
            span = pl.ds(first, chunk)
            swaps.append(swap(right_put.at[span], right_got.at[span], step))
    def outgoing(turn, step, carry):
        first = pl.multiple_of(step * 8 * size, 8 * size)
        sums = [jnp.zeros((depth, chan), jnp.float32) for _ in range(8)]
        for k in range(size):
            rights = right_t[k * size + turn * depth:k * size + (turn + 1) * depth, :]
            for index in range(8):
                sums[index] += left[pl.ds(first + index * size + k, 1), :] * rights
        lead = core * rows if turn == 0 else (1 - core) * rows
        count = ranks // 2
        for index in range(8):
            for row in range(rows):
                at = first + index * size + lead + row
                tri[pl.ds(at, count, stride=2 * rows), :] = sums[index][row * count:(row + 1) * count]
        return carry

    lax.fori_loop(0, depth // 8, functools.partial(outgoing, 0), 0, unroll=True)
    for step in range(spans):
        swaps[step].wait_recv()
        first = pl.multiple_of((here + step) % spans * chunk, chunk)
        spread(right_got[pl.ds(first, chunk), :].astype(jnp.float32), first, 1)
    lax.fori_loop(0, depth // 8, functools.partial(outgoing, 1), 0, unroll=True)

    swaps = []
    for begin in range(0, half, CHUNK):
        span = slice(begin, begin + CHUNK)
        tri_normed = norm_rows(tri[span, :], gains[0][1], False)
        middle = pair_half[span, :].astype(jnp.float32) + gate[span, :] * dot(tri_normed, out_w[0])
        middle = middle.astype(jnp.bfloat16).astype(jnp.float32)
        pair_mid[span, :] = middle
        normed = norm_rows(middle, gains[1][0], True)
        normed_mid[span, :] = normed.astype(jnp.float32)
        rights = dot(normed, jnp.concatenate([side_w[1, 2], side_w[1, 3]], axis=1))
        rights = (sigmoid(rights[:, :chan]) * rights[:, chan:] * pair_mask[span, :]).astype(jnp.bfloat16)
        mid_put[span, :] = rights
        swaps.append(swap(mid_put.at[span], mid_got.at[span], spans + begin // CHUNK))
        right_mid[span, :] = rights.astype(jnp.float32)

    wanted = [pl.ds(rank * rows + index, depth, stride=size) for rank in (sibling, me) for index in range(rows)]
    columns = jnp.concatenate([normed_mid[at, :] for at in wanted], axis=0).astype(jnp.bfloat16)
    column_mask = jnp.concatenate([pair_mask[at, :] for at in wanted], axis=0)
    lefts = dot(columns, jnp.concatenate([side_w[1, 0], side_w[1, 1]], axis=1))
    lefts = (sigmoid(lefts[:, :chan]) * lefts[:, chan:] * column_mask).astype(jnp.bfloat16)
    left_put[...] = lefts[:rows * depth]
    swaps.append(swap(left_put, left_got, spans + half // CHUNK))
    left_own = lefts[rows * depth:].astype(jnp.float32)

    own = pl.ds(pl.multiple_of(slot * block, block), block)
    gate_own = sigmoid(dot(normed_mid[own, :].astype(jnp.bfloat16), side_w[1, 4]))
    sums = [jnp.zeros((size, chan), jnp.float32) for _ in range(rows)]
    for k in range(depth):
        rights = right_mid[k * size:(k + 1) * size, :]
        for index in range(rows):
            sums[index] += left_own[index * depth + k:index * depth + k + 1] * rights
    for copy in swaps:
        copy.wait_recv()
    left_own = left_got[...].astype(jnp.float32)
    for k in range(depth):
        rights = mid_got[k * size:(k + 1) * size, :].astype(jnp.float32)
        for index in range(rows):
            sums[index] += left_own[index * depth + k:index * depth + k + 1] * rights
    tri_normed = norm_rows(jnp.concatenate(sums, axis=0), gains[1][1], False)
    result_ref[...] = (pair_mid[own, :] + gate_own * dot(tri_normed, out_w[1])).astype(jnp.bfloat16)

    for copy in copies:
        copy.wait_send()


def group_body(ranks, pair_rep, residue_mask, side_weights, out_weights, norm_gains):
    rows, size, chan = pair_rep.shape
    half = size * size // 2
    narrow, wide = pltpu.VMEM((half, chan), jnp.bfloat16), pltpu.VMEM((half, chan), jnp.float32)
    edge = pltpu.VMEM((rows * size // 2, chan), jnp.bfloat16)
    swaps = ranks // 4 + half // CHUNK + 1
    result = pl.pallas_call(
        functools.partial(pair_kernel, ranks, size, rows),
        out_shape=pltpu.VMEM((rows * size, chan), jnp.bfloat16),
        in_specs=[pl.BlockSpec(memory_space=pltpu.HBM)] * 5,
        out_specs=pl.BlockSpec(memory_space=pltpu.VMEM),
        scratch_shapes=[
            narrow,
            pltpu.VMEM(side_weights.shape, jnp.bfloat16),
            pltpu.VMEM(out_weights.shape, jnp.bfloat16),
            pltpu.VMEM(norm_gains.shape, jnp.float32),
            pltpu.VMEM((1, size), jnp.int32),
            pltpu.VMEM((size, chan), jnp.float32),
            narrow, narrow, narrow, narrow, edge, edge,
            wide, wide, wide, wide, wide, wide, wide,
            pltpu.VMEM((2 * half, chan), jnp.float32),
            pltpu.SemaphoreType.DMA((ranks // 2,)),
            pltpu.SemaphoreType.DMA((ranks // 2,)),
            pltpu.SemaphoreType.DMA((swaps,)),
            pltpu.SemaphoreType.DMA((swaps,)),
            pltpu.SemaphoreType.DMA((5,)),
        ],
        compiler_params=pltpu.CompilerParams(
            collective_id=0, has_side_effects=True, vmem_limit_bytes=60 << 20
        ),
    )(pair_rep.reshape(rows * size, chan), residue_mask.reshape(1, size), side_weights, out_weights, norm_gains)
    return result.reshape(pair_rep.shape)


def body(ranks, pair_rep, residue_mask, side_weights, out_weights, norm_gains):
    rows, size, chan = pair_rep.shape
    fits = size * size * chan * 4 <= GROUP_BYTES and size * size // 2 % CHUNK == 0 and rows * ranks == size and size % 16 == 0
    if fits and ranks % 4 == 0 and ranks > 4:
        return group_body(ranks, pair_rep, residue_mask, side_weights, out_weights, norm_gains)
    return large_body(pair_rep, residue_mask, side_weights, out_weights, norm_gains)


def solution(mesh):
    in_specs = (P(("grp", "row"), None, None), P("grp"), P(), P(), P())
    out_specs = P(("grp", "row"), None, None)
    mapped = functools.partial(body, mesh.shape["row"])
    return jax.shard_map(mapped, mesh=mesh, in_specs=in_specs, out_specs=out_specs, check_vma=False)
```
